32 devices in a mesh: col: 4 (over x, core), mem: 8 (over z, y).
Axes of the slice: x: 2, y: 2, z: 4, core: 2. Of those that a mesh axis runs over, the one named last changes fastest.
Arguments:
- members: bfloat16 [8, 128, 4096], P('mem', 'col'), may hold values from -15 to 15
- control: bfloat16 [128, 4096], P(None, 'col'), may hold values from -6 to 6
- vertical: bfloat16 [128, 128], replicated, may hold values from -0.5 to 0.5
- blocks: bfloat16 [32, 8, 128, 128], P('col'), may hold values from -0.1875 to 0.1875
- neighbours: int32 [32, 8], P('col'), may hold values from 0 to 31, as said below
- counts: int32 [32], P('col'), may hold values from 4 to 8, as said below
Outputs:
- increment: float32 [128, 4096], P('mem', 'col')
The draws below stay inside these ranges and needn't reach their ends.
Inputs may be any that keep to these rules, and one draw needn't show every extreme that they name: neighbours[p, k] = (p + o) mod 32 with offsets o distinct within a row and -4 <= o <= 4. Entries of neighbours at k >= counts[p] are not used.
All inputs are finite; a program needn't handle non-finite values.
Results may differ from the reference program's by a relative error of at most 0.0041.
Values may be sent and summed in bfloat16 or wider, within the bound.
A program may use at most 64 MiB of HBM per device.

```python
import jax
import jax.numpy as jnp
from jax import lax

LEV = 128
PATCH = 128
NB = 8
REACH = 4
PATCHES = 32
COLS = 4096
MEMBERS = 8


def draw_neighbours(key, part):
    key = jax.random.fold_in(key, 11)
    row_keys = jax.random.split(key, PATCHES)
    offsets = jax.vmap(lambda one_key: jax.random.permutation(one_key, 2 * REACH + 1)[:NB])(row_keys) - REACH
    return ((jnp.arange(PATCHES)[:, None] + offsets) % PATCHES).astype(jnp.int32)


def draw_counts(key, part):
    key = jax.random.fold_in(key, 23)
    drawn = jax.random.randint(key, (PATCHES,), NB // 2, NB + 1)
    return drawn.at[0].set(NB).astype(jnp.int32)


def shard_levels(stream_key, extent, pieces, least, high):
    level, own = 1.0, jax.random.fold_in(stream_key, 6)
    for position, shards_of in pieces:
        draws = jnp.exp(jax.random.uniform(jax.random.fold_in(own, position), (shards_of,), jnp.float32, least / len(pieces), high / len(pieces)))
        level = level * jnp.repeat(draws, extent[position] // shards_of).reshape([-1 if axis == position else 1 for axis in range(len(extent))])
    return level


def bell_draw(stream_key, dims, width, reach, shards=(), held_as=jnp.bfloat16):
    factor_of = shard_levels(stream_key, dims, shards, -0.22, 0.18) if shards else 1.0
    result = jax.random.normal(stream_key, dims, jnp.float32) * width * factor_of
    return jnp.minimum(jnp.maximum(result, -reach), reach).astype(held_as)


def setup_inputs(seed: int = 0) -> dict:
    arg_keys = jax.random.split(jax.random.key(seed), 7)
    members = bell_draw(arg_keys[0], (MEMBERS, LEV, COLS), 3.0, 15.0, ((0, 8), (1, 4)))
    control = bell_draw(arg_keys[1], (LEV, COLS), 1.0, 6.0, ((1, 4),))
    vertical = bell_draw(arg_keys[2], (LEV, LEV), LEV ** -0.5, 0.5)
    blocks = bell_draw(arg_keys[3], (PATCHES, NB, PATCH, PATCH), (PATCH * NB) ** -0.5, 0.1875, ((0, 4),))
    neighbours = draw_neighbours(jax.random.fold_in(arg_keys[6], 71), 0)
    counts = draw_counts(jax.random.fold_in(arg_keys[6], 71), 0)
    return dict(members=members, control=control, vertical=vertical, blocks=blocks, neighbours=neighbours, counts=counts)


def reference(members, control, vertical, blocks, neighbours, counts):
    control_wide = control.astype(jnp.float32)
    blocks_wide = blocks.astype(jnp.float32)
    in_use = (jnp.arange(NB)[None, :] < counts[:, None]).astype(jnp.float32)

    def one_member(carry, slab):
        weighted = (slab.astype(jnp.float32) * control_wide).astype(jnp.bfloat16)
        lifted = jnp.dot(vertical, weighted, preferred_element_type=jnp.float32).astype(jnp.bfloat16)
        patch_grid = lifted.astype(jnp.float32).reshape(LEV, PATCHES, PATCH)
        spread = jnp.zeros((LEV, PATCHES, PATCH), jnp.float32)
        for k in range(NB):
            picked = jnp.take(patch_grid, neighbours[:, k], axis=1) * in_use[:, k][None, :, None]
            spread = spread + jnp.einsum('lpc,pdc->lpd', picked, blocks_wide[:, k])
        member_term = slab.astype(jnp.float32) * spread.reshape(LEV, COLS)
        return carry + member_term, None

    total, unused = lax.scan(one_member, jnp.zeros((LEV, COLS), jnp.float32), members)
    return total / jnp.float32(MEMBERS - 1)
```

```python
import functools

import jax
import jax.numpy as jnp
from jax import lax
from jax.experimental import pallas as pl
from jax.experimental.pallas import tpu as pltpu
from jax.sharding import PartitionSpec as P

PATCH = 128
REACH = 4
MESH = pl.DeviceIdType.MESH


def kernel(
    ncol, nmem, members, control, vertical, blocks, near_ids, counts, out_ref,
    held, ctl, vert, blk, fields, late, stage, landed,
    load_sem, slab_send, slab_recv, far_send, far_recv, near_send, near_recv, sum_send, sum_recv,
):
    me, mine = lax.axis_index("col"), lax.axis_index("mem")
    first = lax.rem(me, 2)
    second = 1 - first
    levels = vertical.shape[0]
    width = REACH * PATCH
    columns = 2 * width
    share = levels // nmem
    total = ncol * 2 * REACH
    slots = near_ids.shape[1]
    blank = 4 * REACH

    loads = [
        pltpu.make_async_copy(control, ctl, load_sem.at[0]),
        pltpu.make_async_copy(vertical, vert, load_sem.at[1]),
        pltpu.make_async_copy(blocks, blk, load_sem.at[2]),
    ]
    for load in loads:
        load.start()

    barrier = pltpu.get_barrier_semaphore()
    for s in range(1, ncol):
        pl.semaphore_signal(barrier, inc=1, device_id={"col": lax.rem(me + s, ncol)}, device_id_type=MESH)
    for s in range(1, nmem):
        pl.semaphore_signal(barrier, inc=1, device_id={"mem": lax.rem(mine + s, nmem)}, device_id_type=MESH)
    fields[blank] = jnp.zeros((levels, PATCH), fields.dtype)
    pl.semaphore_wait(barrier, ncol + nmem - 2)

    for turn in range(2):
        for s in range(ncol):
            to = lax.rem(me + s, ncol)
            half = lax.rem(to + turn, 2)
            start = pl.multiple_of(to * columns + half * width, width)
            source = members.at[0, :, pl.ds(start, width)]
            if s == 0:
                pltpu.make_async_copy(source, held.at[half, me], slab_recv.at[half]).start()
            else:
                pltpu.make_async_remote_copy(
                    src_ref=source, dst_ref=held.at[half, me],
                    send_sem=slab_send.at[turn], recv_sem=slab_recv.at[half],
                    device_id={"col": to}, device_id_type=MESH,
                ).start()

    def lift(half):
        pltpu.make_async_copy(held.at[half], held.at[half], slab_recv.at[half]).wait()
        slab = held[half].astype(jnp.float32).reshape(levels, width)
        scale = ctl[:, pl.ds(pl.multiple_of(half * width, width), width)].astype(jnp.float32)
        weighted = (slab * scale).astype(jnp.bfloat16)
        lifted = jnp.dot(vert[...], weighted, preferred_element_type=jnp.float32).astype(jnp.bfloat16)
        for q in range(REACH):
            fields[REACH + REACH * half + q] = lifted[:, q * PATCH : (q + 1) * PATCH]

    def spread_patch(half, q):
        patch = half * REACH + q
        own = me * (2 * REACH) + patch
        used = counts[patch]
        tiles = []
        for k in range(slots):
            offset = near_ids[patch, k] - own + REACH
            offset = jnp.where(offset < 0, offset + total, offset)
            offset = jnp.where(offset >= total, offset - total, offset)
            tiles.append(fields[jnp.where(k < used, offset + patch, blank)])
        weights = [blk[patch, k] for k in range(slots)]
        spread = lax.dot_general(
            jnp.concatenate(tiles, axis=1), jnp.concatenate(weights, axis=1),
            (((1,), (1,)), ((), ())), preferred_element_type=jnp.float32,
        )
        slab = held[half, :, :, pl.ds(pl.multiple_of(q * PATCH, PATCH), PATCH)]
        term = slab.astype(jnp.float32).reshape(levels, PATCH) * spread
        term = term.astype(jnp.bfloat16)
        group = half * 2 + q // 2
        place = pl.ds(pl.multiple_of((q % 2) * PATCH, PATCH), PATCH)
        for j in range(nmem):
            stage[group, j, :, place] = term[j * share : (j + 1) * share]

    def send_group(group):
        for s in range(1, nmem):
            to = lax.rem(mine + s, nmem)
            pltpu.make_async_remote_copy(
                src_ref=stage.at[group, to], dst_ref=landed.at[group, mine],
                send_sem=sum_send.at[group], recv_sem=sum_recv.at[group],
                device_id={"mem": to}, device_id_type=MESH,
            ).start()
        landed[group, mine] = stage[group, mine]

    def add_group(group):
        pieces = landed.at[group, pl.ds(0, nmem - 1)]
        pltpu.make_async_copy(pieces, pieces, sum_recv.at[group]).wait()
        summed = jnp.sum(landed[group].astype(jnp.float32), axis=0)
        place = pl.ds(pl.multiple_of(group * 2 * PATCH, 2 * PATCH), 2 * PATCH)
        out_ref[:, place] = summed / jnp.float32(nmem - 1)

    loads[0].wait()
    loads[1].wait()
    lift(first)
    far = []
    for s in range(REACH):
        q = s + first * (REACH - 1 - 2 * s)
        far.append(
            pltpu.make_async_remote_copy(
                src_ref=fields.at[REACH + REACH * first + q], dst_ref=late.at[q],
                send_sem=far_send.at[s], recv_sem=far_recv.at[s],
                device_id={"col": lax.rem(me + ncol + 2 * first - 1, ncol)}, device_id_type=MESH,
            )
        )
        far[-1].start()
    lift(second)
    near = pltpu.make_async_remote_copy(
        src_ref=fields.at[pl.ds(REACH + REACH * second, REACH)],
        dst_ref=fields.at[pl.ds(3 * REACH * first, REACH)],
        send_sem=near_send, recv_sem=near_recv,
        device_id={"col": lax.rem(me + ncol + 2 * second - 1, ncol)}, device_id_type=MESH,
    )
    near.start()
    loads[2].wait()
    near.wait_recv()

    for q in range(REACH):
        spread_patch(second, q)
        if q % 2 == 1:
            send_group(second * 2 + q // 2)

    for s in range(REACH):
        q = s + second * (REACH - 1 - 2 * s)
        far[s].wait_recv()
        fields[3 * REACH * first + q] = late[q]
        spread_patch(first, q)
        if s % 2 == 1:
            send_group(first * 2 + q // 2)

    add_group(second * 2)
    add_group(second * 2 + 1)
    add_group(first * 2 + second)
    add_group(first * 2 + first)

    for turn in range(2):
        pieces = held.at[turn, pl.ds(0, ncol - 1)]
        pltpu.make_async_copy(pieces, pieces, slab_send.at[turn]).wait()
    for copy in far:
        copy.wait_send()
    near.wait_send()
    for group in range(4):
        pieces = stage.at[group, pl.ds(0, nmem - 1)]
        pltpu.make_async_copy(pieces, pieces, sum_send.at[group]).wait()


def solution(mesh):
    ncol, nmem = mesh.shape["col"], mesh.shape["mem"]

    def per_device(members, control, vertical, blocks, neighbours, counts):
        levels, columns = control.shape
        patches, slots = neighbours.shape
        slab_rows = members.shape[1]
        assert members.shape[0] == 1 and patches == 2 * REACH and ncol % 2 == 0
        share = levels // nmem
        bf16 = jnp.bfloat16
        dma = pltpu.SemaphoreType.DMA
        anywhere = pl.BlockSpec(memory_space=pl.ANY)
        scalars = pl.BlockSpec(memory_space=pltpu.SMEM)
        return pl.pallas_call(
            functools.partial(kernel, ncol, nmem),
            out_shape=jax.ShapeDtypeStruct((share, columns), jnp.float32),
            in_specs=[anywhere] * 4 + [scalars] * 2,
            out_specs=pl.BlockSpec(memory_space=pltpu.VMEM),
            scratch_shapes=[
                pltpu.VMEM((2, ncol, slab_rows, columns // 2), bf16),
                pltpu.VMEM((levels, columns), bf16),
                pltpu.VMEM((levels, levels), bf16),
                pltpu.VMEM((patches, slots, PATCH, PATCH), bf16),
                pltpu.VMEM((4 * REACH + 1, levels, PATCH), bf16),
                pltpu.VMEM((REACH, levels, PATCH), bf16),
                pltpu.VMEM((4, nmem, share, 2 * PATCH), bf16),
                pltpu.VMEM((4, nmem, share, 2 * PATCH), bf16),
                dma((3,)), dma((2,)), dma((2,)), dma((REACH,)), dma((REACH,)), dma, dma, dma((4,)), dma((4,)),
            ],
            compiler_params=pltpu.CompilerParams(
                collective_id=0, has_side_effects=True, vmem_limit_bytes=48 * 1024 * 1024
            ),
            name="localized_covariance",
        )(members, control, vertical, blocks, neighbours, counts)

    placed = (
        P("mem", "col", None),
        P(None, "col"),
        P(),
        P("col", None, None, None),
        P("col", None),
        P("col"),
    )
    return jax.shard_map(
        per_device, mesh=mesh, in_specs=placed, out_specs=P("mem", "col"), check_vma=False
    )
```

```python
import functools

import jax
import jax.numpy as jnp
from jax import lax
from jax.experimental import pallas as pl
from jax.experimental.pallas import tpu as pltpu
from jax.sharding import PartitionSpec as P

PATCH = 128
REACH = 4
MESH = pl.DeviceIdType.MESH


def kernel(
    ncol, nmem, members, control, vertical, blocks, neighbours, counts_in, out_ref,
    near_ids, counts, held, ctl, vert, blk, fields, late, stage, landed,
    load_sem, slab_send, slab_recv, far_send, far_recv, near_send, near_recv, sum_send, sum_recv,
):
    me, mine = lax.axis_index("col"), lax.axis_index("mem")
    first = lax.rem(me, 2)
    second = 1 - first
    levels = vertical.shape[0]
    width = REACH * PATCH
    columns = 2 * width
    share = levels // nmem
    total = ncol * 2 * REACH
    slots = near_ids.shape[1]
    blank = 4 * REACH

    loads = [
        pltpu.make_async_copy(control, ctl, load_sem.at[0]),
        pltpu.make_async_copy(vertical, vert, load_sem.at[1]),
        pltpu.make_async_copy(blocks, blk, load_sem.at[2]),
        pltpu.make_async_copy(neighbours, near_ids, load_sem.at[3]),
        pltpu.make_async_copy(counts_in, counts, load_sem.at[4]),
    ]
    for load in loads:
        load.start()

    barrier = pltpu.get_barrier_semaphore()
    for s in range(1, ncol):
        pl.semaphore_signal(barrier, inc=1, device_id={"col": lax.rem(me + s, ncol)}, device_id_type=MESH)
    for s in range(1, nmem):
        pl.semaphore_signal(barrier, inc=1, device_id={"mem": lax.rem(mine + s, nmem)}, device_id_type=MESH)
    fields[blank] = jnp.zeros((levels, PATCH), fields.dtype)
    pl.semaphore_wait(barrier, ncol + nmem - 2)

    for turn in range(2):
        for s in range(ncol):
            to = lax.rem(me + s, ncol)
            half = lax.rem(to + turn, 2)
            start = pl.multiple_of(to * columns + half * width, width)
            source = members.at[0, :, pl.ds(start, width)]
            if s == 0:
                pltpu.make_async_copy(source, held.at[half, me], slab_recv.at[half]).start()
            else:
                pltpu.make_async_remote_copy(
                    src_ref=source, dst_ref=held.at[half, me],
                    send_sem=slab_send.at[turn], recv_sem=slab_recv.at[half],
                    device_id={"col": to}, device_id_type=MESH,
                ).start()

    def lift(half):
        pltpu.make_async_copy(held.at[half], held.at[half], slab_recv.at[half]).wait()
        slab = held[half].astype(jnp.float32).reshape(levels, width)
        scale = ctl[:, pl.ds(pl.multiple_of(half * width, width), width)].astype(jnp.float32)
        weighted = (slab * scale).astype(jnp.bfloat16)
        lifted = jnp.dot(vert[...], weighted, preferred_element_type=jnp.float32).astype(jnp.bfloat16)
        for q in range(REACH):
            fields[REACH + REACH * half + q] = lifted[:, q * PATCH : (q + 1) * PATCH]

    def spread_patch(half, q):
        patch = half * REACH + q
        own = me * (2 * REACH) + patch
        used = counts[patch]
        tiles = []
        for k in range(slots):
            offset = near_ids[patch, k] - own + REACH
            offset = jnp.where(offset < 0, offset + total, offset)
            offset = jnp.where(offset >= total, offset - total, offset)
            tiles.append(fields[jnp.where(k < used, offset + patch, blank)])
        weights = [blk[patch, k] for k in range(slots)]
        spread = lax.dot_general(
            jnp.concatenate(tiles, axis=1), jnp.concatenate(weights, axis=1),
            (((1,), (1,)), ((), ())), preferred_element_type=jnp.float32,
        )
        slab = held[half, :, :, pl.ds(pl.multiple_of(q * PATCH, PATCH), PATCH)]
        term = slab.astype(jnp.float32).reshape(levels, PATCH) * spread
        term = term.astype(jnp.bfloat16)
        group = half * 2 + q // 2
        place = pl.ds(pl.multiple_of((q % 2) * PATCH, PATCH), PATCH)
        for j in range(nmem):
            stage[group, j, :, place] = term[j * share : (j + 1) * share]

    def send_group(group):
        for s in range(1, nmem):
            to = lax.rem(mine + s, nmem)
            pltpu.make_async_remote_copy(
                src_ref=stage.at[group, to], dst_ref=landed.at[group, mine],
                send_sem=sum_send.at[group], recv_sem=sum_recv.at[group],
                device_id={"mem": to}, device_id_type=MESH,
            ).start()
        landed[group, mine] = stage[group, mine]

    def add_group(group):
        pieces = landed.at[group, pl.ds(0, nmem - 1)]
        pltpu.make_async_copy(pieces, pieces, sum_recv.at[group]).wait()
        summed = jnp.sum(landed[group].astype(jnp.float32), axis=0)
        place = pl.ds(pl.multiple_of(group * 2 * PATCH, 2 * PATCH), 2 * PATCH)
        out_ref[:, place] = summed / jnp.float32(nmem - 1)

    loads[0].wait()
    loads[1].wait()
    lift(first)
    far = []
    for s in range(REACH):
        q = s + first * (REACH - 1 - 2 * s)
        far.append(
            pltpu.make_async_remote_copy(
                src_ref=fields.at[REACH + REACH * first + q], dst_ref=late.at[q],
                send_sem=far_send.at[s], recv_sem=far_recv.at[s],
                device_id={"col": lax.rem(me + ncol + 2 * first - 1, ncol)}, device_id_type=MESH,
            )
        )
        far[-1].start()
    lift(second)
    near = pltpu.make_async_remote_copy(
        src_ref=fields.at[pl.ds(REACH + REACH * second, REACH)],
        dst_ref=fields.at[pl.ds(3 * REACH * first, REACH)],
        send_sem=near_send, recv_sem=near_recv,
        device_id={"col": lax.rem(me + ncol + 2 * second - 1, ncol)}, device_id_type=MESH,
    )
    near.start()
    for load in loads[2:]:
        load.wait()
    near.wait_recv()

    for q in range(REACH):
        spread_patch(second, q)
        if q % 2 == 1:
            send_group(second * 2 + q // 2)

    for s in range(REACH):
        q = s + second * (REACH - 1 - 2 * s)
        far[s].wait_recv()
        fields[3 * REACH * first + q] = late[q]
        spread_patch(first, q)
        if s % 2 == 1:
            send_group(first * 2 + q // 2)

    add_group(second * 2)
    add_group(second * 2 + 1)
    add_group(first * 2 + second)
    add_group(first * 2 + first)

    for turn in range(2):
        pieces = held.at[turn, pl.ds(0, ncol - 1)]
        pltpu.make_async_copy(pieces, pieces, slab_send.at[turn]).wait()
    for copy in far:
        copy.wait_send()
    near.wait_send()
    for group in range(4):
        pieces = stage.at[group, pl.ds(0, nmem - 1)]
        pltpu.make_async_copy(pieces, pieces, sum_send.at[group]).wait()


def solution(mesh):
    ncol, nmem = mesh.shape["col"], mesh.shape["mem"]

    def per_device(members, control, vertical, blocks, neighbours, counts):
        levels, columns = control.shape
        patches, slots = neighbours.shape
        slab_rows = members.shape[1]
        assert members.shape[0] == 1 and patches == 2 * REACH and ncol % 2 == 0
        share = levels // nmem
        bf16 = jnp.bfloat16
        dma = pltpu.SemaphoreType.DMA
        in_hbm = pl.BlockSpec(memory_space=pltpu.HBM)
        return pl.pallas_call(
            functools.partial(kernel, ncol, nmem),
            out_shape=jax.ShapeDtypeStruct((share, columns), jnp.float32),
            in_specs=[in_hbm] * 6,
            out_specs=pl.BlockSpec(memory_space=pltpu.VMEM),
            scratch_shapes=[
                pltpu.SMEM((patches, slots), jnp.int32),
                pltpu.SMEM((patches,), jnp.int32),
                pltpu.VMEM((2, ncol, slab_rows, columns // 2), bf16),
                pltpu.VMEM((levels, columns), bf16),
                pltpu.VMEM((levels, levels), bf16),
                pltpu.VMEM((patches, slots, PATCH, PATCH), bf16),
                pltpu.VMEM((4 * REACH + 1, levels, PATCH), bf16),
                pltpu.VMEM((REACH, levels, PATCH), bf16),
                pltpu.VMEM((4, nmem, share, 2 * PATCH), bf16),
                pltpu.VMEM((4, nmem, share, 2 * PATCH), bf16),
                dma((5,)), dma((2,)), dma((2,)), dma((REACH,)), dma((REACH,)), dma, dma, dma((4,)), dma((4,)),
            ],
            compiler_params=pltpu.CompilerParams(
                collective_id=0, has_side_effects=True, vmem_limit_bytes=60 * 1024 * 1024
            ),
            name="localized_covariance",
        )(members, control, vertical, blocks, neighbours, counts)

    placed = (
        P("mem", "col", None),
        P(None, "col"),
        P(),
        P("col", None, None, None),
        P("col", None),
        P("col"),
    )
    return jax.shard_map(
        per_device, mesh=mesh, in_specs=placed, out_specs=P("mem", "col"), check_vma=False
    )
```

```python
import functools

import jax
import jax.numpy as jnp
from jax import lax
from jax.experimental import pallas as pl
from jax.experimental.pallas import tpu as pltpu
from jax.sharding import PartitionSpec as P

PATCH = 128
REACH = 4
MESH = pl.DeviceIdType.MESH


def kernel(
    ncol, nmem, members, control, vertical, blocks, neighbours, counts_in, out_ref,
    near_ids, counts, held, ctl, vert, blk, fields, late, stage, landed,
    load_sem, slab_send, slab_recv, far_send, far_recv, near_send, near_recv, sum_send, sum_recv, joined, ready,
):
    me, mine = lax.axis_index("col"), lax.axis_index("mem")
    first = lax.rem(me, 2)
    second = 1 - first
    levels = vertical.shape[0]
    width = REACH * PATCH
    columns = 2 * width
    share = levels // nmem
    total = ncol * 2 * REACH
    slots = near_ids.shape[1]
    blank = 4 * REACH

    loads = [
        pltpu.make_async_copy(control, ctl, load_sem.at[0]),
        pltpu.make_async_copy(vertical, vert, load_sem.at[1]),
        pltpu.make_async_copy(blocks, blk, load_sem.at[2]),
        pltpu.make_async_copy(neighbours, near_ids, load_sem.at[3]),
        pltpu.make_async_copy(counts_in, counts, load_sem.at[4]),
    ]
    for load in loads:
        load.start()

    barrier = pltpu.get_barrier_semaphore()
    leads = me == 0
    for s in range(1, ncol):
        to = lax.rem(me + s, ncol)

        @pl.when(to != 0)
        def _():
            pl.semaphore_signal(barrier, inc=1, device_id={"col": to}, device_id_type=MESH)

    fields[blank] = jnp.zeros((levels, PATCH), fields.dtype)

    @pl.when(leads)
    def _():
        pl.semaphore_wait(joined, ncol - 1)
        for s in range(1, nmem):
            pl.semaphore_signal(barrier, inc=1, device_id={"mem": lax.rem(mine + s, nmem)}, device_id_type=MESH)

    @pl.when(jnp.logical_not(leads))
    def _():
        pl.semaphore_wait(barrier, ncol - 1)
        pl.semaphore_signal(joined, inc=1, device_id={"col": 0}, device_id_type=MESH)

    for turn in range(2):
        for s in range(ncol):
            to = lax.rem(me + s, ncol)
            half = lax.rem(to + turn, 2)
            start = pl.multiple_of(to * columns + half * width, width)
            source = members.at[0, :, pl.ds(start, width)]
            if s == 0:
                pltpu.make_async_copy(source, held.at[half, me], slab_recv.at[half]).start()
            else:
                pltpu.make_async_remote_copy(
                    src_ref=source, dst_ref=held.at[half, me],
                    send_sem=slab_send.at[turn], recv_sem=slab_recv.at[half],
                    device_id={"col": to}, device_id_type=MESH,
                ).start()

    def lift(half):
        pltpu.make_async_copy(held.at[half], held.at[half], slab_recv.at[half]).wait()
        slab = held[half].astype(jnp.float32).reshape(levels, width)
        scale = ctl[:, pl.ds(pl.multiple_of(half * width, width), width)].astype(jnp.float32)
        weighted = (slab * scale).astype(jnp.bfloat16)
        lifted = jnp.dot(vert[...], weighted, preferred_element_type=jnp.float32).astype(jnp.bfloat16)
        for q in range(REACH):
            fields[REACH + REACH * half + q] = lifted[:, q * PATCH : (q + 1) * PATCH]

    def spread_patch(half, q):
        patch = half * REACH + q
        own = me * (2 * REACH) + patch
        used = counts[patch]
        tiles = []
        for k in range(slots):
            offset = near_ids[patch, k] - own + REACH
            offset = jnp.where(offset < 0, offset + total, offset)
            offset = jnp.where(offset >= total, offset - total, offset)
            tiles.append(fields[jnp.where(k < used, offset + patch, blank)])
        weights = [blk[patch, k] for k in range(slots)]
        spread = lax.dot_general(
            jnp.concatenate(tiles, axis=1), jnp.concatenate(weights, axis=1),
            (((1,), (1,)), ((), ())), preferred_element_type=jnp.float32,
        )
        slab = held[half, :, :, pl.ds(pl.multiple_of(q * PATCH, PATCH), PATCH)]
        term = slab.astype(jnp.float32).reshape(levels, PATCH) * spread
        term = term.astype(jnp.bfloat16)
        group = half * 2 + q // 2
        place = pl.ds(pl.multiple_of((q % 2) * PATCH, PATCH), PATCH)
        for j in range(nmem):
            stage[group, j, :, place] = term[j * share : (j + 1) * share]

    def send_group(group):
        for s in range(1, nmem):
            to = lax.rem(mine + s, nmem)
            pltpu.make_async_remote_copy(
                src_ref=stage.at[group, to], dst_ref=landed.at[group, mine],
                send_sem=sum_send.at[group], recv_sem=sum_recv.at[group],
                device_id={"mem": to}, device_id_type=MESH,
            ).start()
        landed[group, mine] = stage[group, mine]

    def add_group(group):
        pieces = landed.at[group, pl.ds(0, nmem - 1)]
        pltpu.make_async_copy(pieces, pieces, sum_recv.at[group]).wait()
        summed = jnp.sum(landed[group].astype(jnp.float32), axis=0)
        place = pl.ds(pl.multiple_of(group * 2 * PATCH, 2 * PATCH), 2 * PATCH)
        out_ref[:, place] = summed / jnp.float32(nmem - 1)

    loads[0].wait()
    loads[1].wait()
    lift(first)
    far = []
    for s in range(REACH):
        q = s + first * (REACH - 1 - 2 * s)
        far.append(
            pltpu.make_async_remote_copy(
                src_ref=fields.at[REACH + REACH * first + q], dst_ref=late.at[q],
                send_sem=far_send.at[s], recv_sem=far_recv.at[s],
                device_id={"col": lax.rem(me + ncol + 2 * first - 1, ncol)}, device_id_type=MESH,
            )
        )
        far[-1].start()
    lift(second)
    near = pltpu.make_async_remote_copy(
        src_ref=fields.at[pl.ds(REACH + REACH * second, REACH)],
        dst_ref=fields.at[pl.ds(3 * REACH * first, REACH)],
        send_sem=near_send, recv_sem=near_recv,
        device_id={"col": lax.rem(me + ncol + 2 * second - 1, ncol)}, device_id_type=MESH,
    )
    near.start()

    @pl.when(leads)
    def _():
        pl.semaphore_wait(barrier, nmem - 1)
        for s in range(1, ncol):
            pl.semaphore_signal(ready, inc=1, device_id={"col": lax.rem(me + s, ncol)}, device_id_type=MESH)

    for load in loads[2:]:
        load.wait()
    near.wait_recv()

    @pl.when(jnp.logical_not(leads))
    def _():
        pl.semaphore_wait(ready, 1)

    for q in range(REACH):
        spread_patch(second, q)
        if q % 2 == 1:
            send_group(second * 2 + q // 2)

    for s in range(REACH):
        q = s + second * (REACH - 1 - 2 * s)
        far[s].wait_recv()
        fields[3 * REACH * first + q] = late[q]
        spread_patch(first, q)
        if s % 2 == 1:
            send_group(first * 2 + q // 2)

    add_group(second * 2)
    add_group(second * 2 + 1)
    add_group(first * 2 + second)
    add_group(first * 2 + first)

    for turn in range(2):
        pieces = held.at[turn, pl.ds(0, ncol - 1)]
        pltpu.make_async_copy(pieces, pieces, slab_send.at[turn]).wait()
    for copy in far:
        copy.wait_send()
    near.wait_send()
    for group in range(4):
        pieces = stage.at[group, pl.ds(0, nmem - 1)]
        pltpu.make_async_copy(pieces, pieces, sum_send.at[group]).wait()


def solution(mesh):
    ncol, nmem = mesh.shape["col"], mesh.shape["mem"]

    def per_device(members, control, vertical, blocks, neighbours, counts):
        levels, columns = control.shape
        patches, slots = neighbours.shape
        slab_rows = members.shape[1]
        assert members.shape[0] == 1 and patches == 2 * REACH and ncol % 2 == 0
        share = levels // nmem
        bf16 = jnp.bfloat16
        dma = pltpu.SemaphoreType.DMA
        in_hbm = pl.BlockSpec(memory_space=pltpu.HBM)
        return pl.pallas_call(
            functools.partial(kernel, ncol, nmem),
            out_shape=jax.ShapeDtypeStruct((share, columns), jnp.float32),
            in_specs=[in_hbm] * 6,
            out_specs=pl.BlockSpec(memory_space=pltpu.VMEM),
            scratch_shapes=[
                pltpu.SMEM((patches, slots), jnp.int32),
                pltpu.SMEM((patches,), jnp.int32),
                pltpu.VMEM((2, ncol, slab_rows, columns // 2), bf16),
                pltpu.VMEM((levels, columns), bf16),
                pltpu.VMEM((levels, levels), bf16),
                pltpu.VMEM((patches, slots, PATCH, PATCH), bf16),
                pltpu.VMEM((4 * REACH + 1, levels, PATCH), bf16),
                pltpu.VMEM((REACH, levels, PATCH), bf16),
                pltpu.VMEM((4, nmem, share, 2 * PATCH), bf16),
                pltpu.VMEM((4, nmem, share, 2 * PATCH), bf16),
                dma((5,)), dma((2,)), dma((2,)), dma((REACH,)), dma((REACH,)), dma, dma, dma((4,)), dma((4,)),
                pltpu.SemaphoreType.REGULAR, pltpu.SemaphoreType.REGULAR,
            ],
            compiler_params=pltpu.CompilerParams(
                collective_id=0, has_side_effects=True, vmem_limit_bytes=60 * 1024 * 1024
            ),
            name="localized_covariance",
        )(members, control, vertical, blocks, neighbours, counts)

    placed = (
        P("mem", "col", None),
        P(None, "col"),
        P(),
        P("col", None, None, None),
        P("col", None),
        P("col"),
    )
    return jax.shard_map(
        per_device, mesh=mesh, in_specs=placed, out_specs=P("mem", "col"), check_vma=False
    )
```

```python
import functools

import jax
import jax.numpy as jnp
from jax import lax
from jax.experimental import pallas as pl
from jax.experimental.pallas import tpu as pltpu
from jax.sharding import PartitionSpec as P

PATCH = 128
REACH = 4
MESH = pl.DeviceIdType.MESH


def kernel(
    ncol, nmem, members, control, vertical, blocks, neighbours, counts_in, out_ref,
    near_ids, counts, held, ctl, vert, blk, fields, late, stage, landed,
    load_sem, slab_send, slab_recv, far_send, far_recv, near_send, near_recv, sum_send, sum_recv, joined, ready,
):
    me, mine = lax.axis_index("col"), lax.axis_index("mem")
    first = lax.rem(me, 2)
    second = 1 - first
    levels = vertical.shape[0]
    width = REACH * PATCH
    columns = 2 * width
    share = levels // nmem
    total = ncol * 2 * REACH
    slots = near_ids.shape[1]
    blank = 4 * REACH

    loads = [
        pltpu.make_async_copy(control, ctl, load_sem.at[0]),
        pltpu.make_async_copy(vertical, vert, load_sem.at[1]),
        pltpu.make_async_copy(blocks, blk, load_sem.at[2]),
        pltpu.make_async_copy(neighbours, near_ids, load_sem.at[3]),
        pltpu.make_async_copy(counts_in, counts, load_sem.at[4]),
    ]
    for load in loads:
        load.start()

    barrier = pltpu.get_barrier_semaphore()
    leads = me == 0
    for s in range(1, ncol):
        to = lax.rem(me + s, ncol)

        @pl.when(to != 0)
        def _():
            pl.semaphore_signal(barrier, inc=1, device_id={"col": to}, device_id_type=MESH)

    fields[blank] = jnp.zeros((levels, PATCH), fields.dtype)

    @pl.when(leads)
    def _():
        pl.semaphore_wait(joined, ncol - 1)
        for s in range(1, nmem):
            pl.semaphore_signal(barrier, inc=1, device_id={"mem": lax.rem(mine + s, nmem)}, device_id_type=MESH)

    @pl.when(jnp.logical_not(leads))
    def _():
        pl.semaphore_wait(barrier, ncol - 1)
        pl.semaphore_signal(joined, inc=1, device_id={"col": 0}, device_id_type=MESH)

    for turn in range(2):
        for s in range(ncol):
            to = lax.rem(me + s, ncol)
            half = lax.rem(to + turn, 2)
            start = pl.multiple_of(to * columns + half * width, width)
            source = members.at[0, :, pl.ds(start, width)]
            if s == 0:
                pltpu.make_async_copy(source, held.at[half, me], slab_recv.at[half]).start()
            else:
                pltpu.make_async_remote_copy(
                    src_ref=source, dst_ref=held.at[half, me],
                    send_sem=slab_send.at[turn], recv_sem=slab_recv.at[half],
                    device_id={"col": to}, device_id_type=MESH,
                ).start()

    def lift(half):
        pltpu.make_async_copy(held.at[half], held.at[half], slab_recv.at[half]).wait()
        slab = held[half].astype(jnp.float32).reshape(levels, width)
        scale = ctl[:, pl.ds(pl.multiple_of(half * width, width), width)].astype(jnp.float32)
        weighted = (slab * scale).astype(jnp.bfloat16)
        lifted = jnp.dot(vert[...], weighted, preferred_element_type=jnp.float32).astype(jnp.bfloat16)
        for q in range(REACH):
            fields[REACH + REACH * half + q] = lifted[:, q * PATCH : (q + 1) * PATCH]

    def spread_patch(half, q):
        patch = half * REACH + q
        own = me * (2 * REACH) + patch
        used = counts[patch]
        tiles = []
        for k in range(slots):
            offset = near_ids[patch, k] - own + REACH
            offset = jnp.where(offset < 0, offset + total, offset)
            offset = jnp.where(offset >= total, offset - total, offset)
            tiles.append(fields[jnp.where(k < used, offset + patch, blank)])
        weights = [blk[patch, k] for k in range(slots)]
        spread = lax.dot_general(
            jnp.concatenate(tiles, axis=1), jnp.concatenate(weights, axis=1),
            (((1,), (1,)), ((), ())), preferred_element_type=jnp.float32,
        )
        slab = held[half, :, :, pl.ds(pl.multiple_of(q * PATCH, PATCH), PATCH)]
        term = slab.astype(jnp.float32).reshape(levels, PATCH) * spread
        term = term.astype(jnp.bfloat16)
        group = half
        place = pl.ds(pl.multiple_of(q * PATCH, PATCH), PATCH)
        for j in range(nmem):
            stage[group, j, :, place] = term[j * share : (j + 1) * share]

    def send_group(group):
        for s in range(1, nmem):
            to = lax.rem(mine + s, nmem)
            pltpu.make_async_remote_copy(
                src_ref=stage.at[group, to], dst_ref=landed.at[group, mine],
                send_sem=sum_send.at[group], recv_sem=sum_recv.at[group],
                device_id={"mem": to}, device_id_type=MESH,
            ).start()
        landed[group, mine] = stage[group, mine]

    def add_group(group):
        pieces = landed.at[group, pl.ds(0, nmem - 1)]
        pltpu.make_async_copy(pieces, pieces, sum_recv.at[group]).wait()
        summed = jnp.sum(landed[group].astype(jnp.float32), axis=0)
        place = pl.ds(pl.multiple_of(group * width, width), width)
        out_ref[:, place] = summed / jnp.float32(nmem - 1)

    loads[0].wait()
    loads[1].wait()
    lift(first)
    far = []
    for s in range(REACH):
        q = s + first * (REACH - 1 - 2 * s)
        far.append(
            pltpu.make_async_remote_copy(
                src_ref=fields.at[REACH + REACH * first + q], dst_ref=late.at[q],
                send_sem=far_send.at[s], recv_sem=far_recv.at[s],
                device_id={"col": lax.rem(me + ncol + 2 * first - 1, ncol)}, device_id_type=MESH,
            )
        )
        far[-1].start()
    lift(second)
    near = pltpu.make_async_remote_copy(
        src_ref=fields.at[pl.ds(REACH + REACH * second, REACH)],
        dst_ref=fields.at[pl.ds(3 * REACH * first, REACH)],
        send_sem=near_send, recv_sem=near_recv,
        device_id={"col": lax.rem(me + ncol + 2 * second - 1, ncol)}, device_id_type=MESH,
    )
    near.start()

    @pl.when(leads)
    def _():
        pl.semaphore_wait(barrier, nmem - 1)
        for s in range(1, ncol):
            pl.semaphore_signal(ready, inc=1, device_id={"col": lax.rem(me + s, ncol)}, device_id_type=MESH)

    for load in loads[2:]:
        load.wait()
    near.wait_recv()

    @pl.when(jnp.logical_not(leads))
    def _():
        pl.semaphore_wait(ready, 1)

    for q in range(REACH):
        spread_patch(second, q)
        if q == REACH - 1:
            send_group(second)

    for s in range(REACH):
        q = s + second * (REACH - 1 - 2 * s)
        far[s].wait_recv()
        fields[3 * REACH * first + q] = late[q]
        spread_patch(first, q)
        if s == REACH - 1:
            send_group(first)

    add_group(second)
    add_group(first)

    for turn in range(2):
        pieces = held.at[turn, pl.ds(0, ncol - 1)]
        pltpu.make_async_copy(pieces, pieces, slab_send.at[turn]).wait()
    for copy in far:
        copy.wait_send()
    near.wait_send()
    for group in range(2):
        pieces = stage.at[group, pl.ds(0, nmem - 1)]
        pltpu.make_async_copy(pieces, pieces, sum_send.at[group]).wait()


def solution(mesh):
    ncol, nmem = mesh.shape["col"], mesh.shape["mem"]

    def per_device(members, control, vertical, blocks, neighbours, counts):
        levels, columns = control.shape
        patches, slots = neighbours.shape
        slab_rows = members.shape[1]
        assert members.shape[0] == 1 and patches == 2 * REACH and ncol % 2 == 0
        share = levels // nmem
        bf16 = jnp.bfloat16
        dma = pltpu.SemaphoreType.DMA
        in_hbm = pl.BlockSpec(memory_space=pltpu.HBM)
        return pl.pallas_call(
            functools.partial(kernel, ncol, nmem),
            out_shape=jax.ShapeDtypeStruct((share, columns), jnp.float32),
            in_specs=[in_hbm] * 6,
            out_specs=pl.BlockSpec(memory_space=pltpu.VMEM),
            scratch_shapes=[
                pltpu.SMEM((patches, slots), jnp.int32),
                pltpu.SMEM((patches,), jnp.int32),
                pltpu.VMEM((2, ncol, slab_rows, columns // 2), bf16),
                pltpu.VMEM((levels, columns), bf16),
                pltpu.VMEM((levels, levels), bf16),
                pltpu.VMEM((patches, slots, PATCH, PATCH), bf16),
                pltpu.VMEM((4 * REACH + 1, levels, PATCH), bf16),
                pltpu.VMEM((REACH, levels, PATCH), bf16),
                pltpu.VMEM((2, nmem, share, REACH * PATCH), bf16),
                pltpu.VMEM((2, nmem, share, REACH * PATCH), bf16),
                dma((5,)), dma((2,)), dma((2,)), dma((REACH,)), dma((REACH,)), dma, dma, dma((2,)), dma((2,)),
                pltpu.SemaphoreType.REGULAR, pltpu.SemaphoreType.REGULAR,
            ],
            compiler_params=pltpu.CompilerParams(
                collective_id=0, has_side_effects=True, vmem_limit_bytes=48 * 1024 * 1024
            ),
            name="localized_covariance",
        )(*[pltpu.with_memory_space_constraint(x, pltpu.HBM) for x in (members, control, vertical, blocks, neighbours, counts)])

    placed = (
        P("mem", "col", None),
        P(None, "col"),
        P(),
        P("col", None, None, None),
        P("col", None),
        P("col"),
    )
    return jax.shard_map(
        per_device, mesh=mesh, in_specs=placed, out_specs=P("mem", "col"), check_vma=False
    )
```

```python
import functools

import jax
import jax.numpy as jnp
from jax import lax
from jax.experimental import pallas as pl
from jax.experimental.pallas import tpu as pltpu
from jax.sharding import PartitionSpec as P

PATCH = 128
REACH = 4
MESH = pl.DeviceIdType.MESH


def kernel(
    ncol, nmem, members, control, vertical, blocks, neighbours, counts_in, out_ref,
    slabs, near_ids, counts, held, ctl, vert, blk, fields, late, stage, landed,
    load_sem, slab_send, slab_recv, far_send, far_recv, near_send, near_recv, sum_send, sum_recv, joined, ready,
):
    me, mine = lax.axis_index("col"), lax.axis_index("mem")
    first = lax.rem(me, 2)
    second = 1 - first
    levels = vertical.shape[0]
    width = REACH * PATCH
    columns = 2 * width
    share = levels // nmem
    total = ncol * 2 * REACH
    slots = near_ids.shape[1]
    blank = 4 * REACH

    loads = [
        pltpu.make_async_copy(control, ctl, load_sem.at[0]),
        pltpu.make_async_copy(vertical, vert, load_sem.at[1]),
        pltpu.make_async_copy(blocks, blk, load_sem.at[2]),
        pltpu.make_async_copy(neighbours, near_ids, load_sem.at[3]),
        pltpu.make_async_copy(counts_in, counts, load_sem.at[4]),
    ]
    bring = pltpu.make_async_copy(members, slabs, load_sem.at[5])
    bring.start()
    for load in loads:
        load.start()

    barrier = pltpu.get_barrier_semaphore()
    leads = me == 0
    for s in range(1, ncol):
        to = lax.rem(me + s, ncol)

        @pl.when(to != 0)
        def _():
            pl.semaphore_signal(barrier, inc=1, device_id={"col": to}, device_id_type=MESH)

    fields[blank] = jnp.zeros((levels, PATCH), fields.dtype)

    @pl.when(leads)
    def _():
        pl.semaphore_wait(joined, ncol - 1)
        for s in range(1, nmem):
            pl.semaphore_signal(barrier, inc=1, device_id={"mem": lax.rem(mine + s, nmem)}, device_id_type=MESH)

    @pl.when(jnp.logical_not(leads))
    def _():
        pl.semaphore_wait(barrier, ncol - 1)
        pl.semaphore_signal(joined, inc=1, device_id={"col": 0}, device_id_type=MESH)

    bring.wait()

    for turn in range(2):
        for s in range(ncol):
            to = lax.rem(me + s, ncol)
            half = lax.rem(to + turn, 2)
            start = pl.multiple_of(to * columns + half * width, width)
            source = slabs.at[0, :, pl.ds(start, width)]
            if s == 0:
                pltpu.make_async_copy(source, held.at[half, me], slab_recv.at[half]).start()
            else:
                pltpu.make_async_remote_copy(
                    src_ref=source, dst_ref=held.at[half, me],
                    send_sem=slab_send.at[turn], recv_sem=slab_recv.at[half],
                    device_id={"col": to}, device_id_type=MESH,
                ).start()

    def lift(half):
        pltpu.make_async_copy(held.at[half], held.at[half], slab_recv.at[half]).wait()
        slab = held[half].astype(jnp.float32).reshape(levels, width)
        scale = ctl[:, pl.ds(pl.multiple_of(half * width, width), width)].astype(jnp.float32)
        weighted = (slab * scale).astype(jnp.bfloat16)
        lifted = jnp.dot(vert[...], weighted, preferred_element_type=jnp.float32).astype(jnp.bfloat16)
        for q in range(REACH):
            fields[REACH + REACH * half + q] = lifted[:, q * PATCH : (q + 1) * PATCH]

    def spread_patch(half, q):
        patch = half * REACH + q
        own = me * (2 * REACH) + patch
        used = counts[patch]
        tiles = []
        for k in range(slots):
            offset = near_ids[patch, k] - own + REACH
            offset = jnp.where(offset < 0, offset + total, offset)
            offset = jnp.where(offset >= total, offset - total, offset)
            tiles.append(fields[jnp.where(k < used, offset + patch, blank)])
        weights = [blk[patch, k] for k in range(slots)]
        spread = lax.dot_general(
            jnp.concatenate(tiles, axis=1), jnp.concatenate(weights, axis=1),
            (((1,), (1,)), ((), ())), preferred_element_type=jnp.float32,
        )
        slab = held[half, :, :, pl.ds(pl.multiple_of(q * PATCH, PATCH), PATCH)]
        term = slab.astype(jnp.float32).reshape(levels, PATCH) * spread
        term = term.astype(jnp.bfloat16)
        group = half
        place = pl.ds(pl.multiple_of(q * PATCH, PATCH), PATCH)
        for j in range(nmem):
            stage[group, j, :, place] = term[j * share : (j + 1) * share]

    def send_group(group):
        for s in range(1, nmem):
            to = lax.rem(mine + s, nmem)
            pltpu.make_async_remote_copy(
                src_ref=stage.at[group, to], dst_ref=landed.at[group, mine],
                send_sem=sum_send.at[group], recv_sem=sum_recv.at[group],
                device_id={"mem": to}, device_id_type=MESH,
            ).start()
        landed[group, mine] = stage[group, mine]

    def add_group(group):
        pieces = landed.at[group, pl.ds(0, nmem - 1)]
        pltpu.make_async_copy(pieces, pieces, sum_recv.at[group]).wait()
        summed = jnp.sum(landed[group].astype(jnp.float32), axis=0)
        place = pl.ds(pl.multiple_of(group * width, width), width)
        out_ref[:, place] = summed / jnp.float32(nmem - 1)

    loads[0].wait()
    loads[1].wait()
    lift(first)
    far = []
    for s in range(REACH):
        q = s + first * (REACH - 1 - 2 * s)
        far.append(
            pltpu.make_async_remote_copy(
                src_ref=fields.at[REACH + REACH * first + q], dst_ref=late.at[q],
                send_sem=far_send.at[s], recv_sem=far_recv.at[s],
                device_id={"col": lax.rem(me + ncol + 2 * first - 1, ncol)}, device_id_type=MESH,
            )
        )
        far[-1].start()
    lift(second)
    near = pltpu.make_async_remote_copy(
        src_ref=fields.at[pl.ds(REACH + REACH * second, REACH)],
        dst_ref=fields.at[pl.ds(3 * REACH * first, REACH)],
        send_sem=near_send, recv_sem=near_recv,
        device_id={"col": lax.rem(me + ncol + 2 * second - 1, ncol)}, device_id_type=MESH,
    )
    near.start()

    @pl.when(leads)
    def _():
        pl.semaphore_wait(barrier, nmem - 1)
        for s in range(1, ncol):
            pl.semaphore_signal(ready, inc=1, device_id={"col": lax.rem(me + s, ncol)}, device_id_type=MESH)

    for load in loads[2:]:
        load.wait()
    near.wait_recv()

    @pl.when(jnp.logical_not(leads))
    def _():
        pl.semaphore_wait(ready, 1)

    for q in range(REACH):
        spread_patch(second, q)
        if q == REACH - 1:
            send_group(second)

    for s in range(REACH):
        q = s + second * (REACH - 1 - 2 * s)
        far[s].wait_recv()
        fields[3 * REACH * first + q] = late[q]
        spread_patch(first, q)
        if s == REACH - 1:
            send_group(first)

    add_group(second)
    add_group(first)

    for turn in range(2):
        pieces = held.at[turn, pl.ds(0, ncol - 1)]
        pltpu.make_async_copy(pieces, pieces, slab_send.at[turn]).wait()
    for copy in far:
        copy.wait_send()
    near.wait_send()
    for group in range(2):
        pieces = stage.at[group, pl.ds(0, nmem - 1)]
        pltpu.make_async_copy(pieces, pieces, sum_send.at[group]).wait()


def solution(mesh):
    ncol, nmem = mesh.shape["col"], mesh.shape["mem"]

    def per_device(members, control, vertical, blocks, neighbours, counts):
        levels, columns = control.shape
        patches, slots = neighbours.shape
        slab_rows = members.shape[1]
        assert members.shape[0] == 1 and patches == 2 * REACH and ncol % 2 == 0
        share = levels // nmem
        bf16 = jnp.bfloat16
        dma = pltpu.SemaphoreType.DMA
        in_hbm = pl.BlockSpec(memory_space=pltpu.HBM)
        return pl.pallas_call(
            functools.partial(kernel, ncol, nmem),
            out_shape=jax.ShapeDtypeStruct((share, columns), jnp.float32),
            in_specs=[in_hbm] * 6,
            out_specs=pl.BlockSpec(memory_space=pltpu.VMEM),
            scratch_shapes=[
                pltpu.VMEM(members.shape, bf16),
                pltpu.SMEM((patches, slots), jnp.int32),
                pltpu.SMEM((patches,), jnp.int32),
                pltpu.VMEM((2, ncol, slab_rows, columns // 2), bf16),
                pltpu.VMEM((levels, columns), bf16),
                pltpu.VMEM((levels, levels), bf16),
                pltpu.VMEM((patches, slots, PATCH, PATCH), bf16),
                pltpu.VMEM((4 * REACH + 1, levels, PATCH), bf16),
                pltpu.VMEM((REACH, levels, PATCH), bf16),
                pltpu.VMEM((2, nmem, share, REACH * PATCH), bf16),
                pltpu.VMEM((2, nmem, share, REACH * PATCH), bf16),
                dma((6,)), dma((2,)), dma((2,)), dma((REACH,)), dma((REACH,)), dma, dma, dma((2,)), dma((2,)),
                pltpu.SemaphoreType.REGULAR, pltpu.SemaphoreType.REGULAR,
            ],
            compiler_params=pltpu.CompilerParams(
                collective_id=0, has_side_effects=True, vmem_limit_bytes=48 * 1024 * 1024
            ),
            name="localized_covariance",
        )(*[pltpu.with_memory_space_constraint(x, pltpu.HBM) for x in (members, control, vertical, blocks, neighbours, counts)])

    placed = (
        P("mem", "col", None),
        P(None, "col"),
        P(),
        P("col", None, None, None),
        P("col", None),
        P("col"),
    )
    return jax.shard_map(
        per_device, mesh=mesh, in_specs=placed, out_specs=P("mem", "col"), check_vma=False
    )
```
